256 devices in a mesh: lsec: 16 (over x, z_lo), rsec: 16 (over z_hi, y, core).
Axes of the slice: x: 4, y: 4, z: 8 (z_hi: 2, z_lo: 4; z = z_hi * 4 + z_lo), core: 2. Of those that a mesh axis runs over, the one named last changes fastest.
Arguments:
- states: float32 [2, 10240, 10240], P(None, 'lsec', 'rsec'), may hold values from -6 to 6
- left_env: float32 [16, 640, 640], P('lsec', 'rsec'), may hold values from -0.25 to 0.25
- right_env: float32 [16, 640, 640], P('rsec', 'lsec'), may hold values from -0.25 to 0.25
- left_op: float32 [16, 640, 640], P('lsec', 'rsec'), may hold values from -0.25 to 0.25
- right_op: float32 [16, 640, 640], P('rsec', 'lsec'), may hold values from -0.25 to 0.25
- sizes_left: int32 [16], P('lsec'), may hold values from 320 to 640
- sizes_right: int32 [16], P('rsec'), may hold values from 320 to 640
Outputs:
- applied: float32 [2, 10240, 10240], P(None, 'lsec', 'rsec')
The draws below stay inside these ranges and needn't reach their ends.
All inputs are finite; a program needn't handle non-finite values.
Results may differ from the reference program's by a relative error of at most 0.000059.
Values sent between devices are 32-bit elements; how exact they have to be, the bound alone decides.
A program may use at most 128 MiB of HBM per device.

```python
import jax
import jax.numpy as jnp
from jax import lax

CAP = 640
ROOTS = 2
SEC_L = 16
SEC_R = 16


def touch_ends(array, rng, smallest, largest):
    place = [jax.random.randint(jax.random.fold_in(rng, axis), (), 0, length) for axis, length in enumerate(array.shape)]
    main_axis = array.shape.index(max(array.shape))
    beside = place[:main_axis] + [(place[main_axis] + 1) % array.shape[main_axis]] + place[main_axis + 1:]
    return array.at[tuple(place)].set(smallest).at[tuple(beside)].set(largest)


def block_scale(stream_key, extent, pieces, least, high):
    gain = 1.0
    for position, parts in pieces:
        draws = jax.random.uniform(jax.random.fold_in(jax.random.fold_in(stream_key, 6), position), (parts,), jnp.float32, least / len(pieces), high / len(pieces))
        gain = gain * jnp.repeat(jnp.exp(draws), extent[position] // parts).reshape((-1,) + (1,) * (len(extent) - 1 - position))
    return gain


def noise(own_key, dims, spread, limit, shards=(), kind=jnp.bfloat16):
    drawn = jax.random.normal(own_key, dims, jnp.float32) * spread
    if len(shards) > 0:
        drawn = block_scale(own_key, dims, shards, -0.22, 0.18) * drawn
    return jnp.clip(drawn, min=-limit, max=limit).astype(kind)


def setup_inputs(seed: int = 0) -> dict:
    key_of = jax.random.split(jax.random.key(seed), 8)
    states = noise(key_of[0], (ROOTS, SEC_L * CAP, SEC_R * CAP), 1.0, 6.0, ((1, 16), (2, 16)), jnp.float32)
    left_env = noise(key_of[1], (SEC_L, CAP, CAP), CAP ** -0.5, 0.25, ((0, 16), (1, 16)), jnp.float32)
    right_env = noise(key_of[2], (SEC_R, CAP, CAP), CAP ** -0.5, 0.25, ((0, 16), (1, 16)), jnp.float32)
    left_op = noise(key_of[3], (SEC_L, CAP, CAP), CAP ** -0.5, 0.25, ((0, 16), (1, 16)), jnp.float32)
    right_op = noise(key_of[4], (SEC_R, CAP, CAP), CAP ** -0.5, 0.25, ((0, 16), (1, 16)), jnp.float32)
    sizes_left = touch_ends(jax.random.randint(key_of[5], (SEC_L,), CAP // 2, CAP + 1), jax.random.fold_in(key_of[5], 1), CAP // 2, CAP).astype(jnp.int32)
    sizes_right = touch_ends(jax.random.randint(key_of[6], (SEC_R,), CAP // 2, CAP + 1), jax.random.fold_in(key_of[6], 1), CAP // 2, CAP).astype(jnp.int32)
    return dict(states=states, left_env=left_env, right_env=right_env, left_op=left_op, right_op=right_op, sizes_left=sizes_left, sizes_right=sizes_right)


HI = lax.Precision.HIGHEST


def reference(states, left_env, right_env, left_op, right_op, sizes_left, sizes_right):
    rows = jnp.arange(CAP, dtype=jnp.int32)
    mask_l = (rows[None, :] < sizes_left[:, None]).astype(jnp.float32)
    mask_r = (rows[None, :] < sizes_right[:, None]).astype(jnp.float32)
    mask = mask_l[:, :, None, None] * mask_r[None, None, :, :]
    blocks = states.reshape(ROOTS, SEC_L, CAP, SEC_R, CAP) * mask[None]
    local = jnp.einsum('iab,ribjc->riajc', left_env, blocks, precision=HI)
    local = local + jnp.einsum('ribjc,jdc->ribjd', blocks, right_env, precision=HI)
    moved = jnp.pad(blocks[:, :-1, :, 1:, :], ((0, 0), (1, 0), (0, 0), (0, 1), (0, 0)))
    inner = jnp.einsum('ribjc,jdc->ribjd', moved, right_op, precision=HI)
    hop = jnp.einsum('iab,ribjd->riajd', left_op, inner, precision=HI)
    right_part = jnp.einsum('ribjc,jcd->ribjd', blocks, right_op, precision=HI)
    source = jnp.einsum('iba,ribjd->riajd', left_op, right_part, precision=HI)
    back = jnp.pad(source[:, 1:, :, :-1, :], ((0, 0), (0, 1), (0, 0), (1, 0), (0, 0)))
    applied = (local + hop + back) * mask[None]
    return applied.reshape(ROOTS, SEC_L * CAP, SEC_R * CAP)
```

```python
import jax
import jax.numpy as jnp
from jax import lax
from jax.sharding import PartitionSpec as P

HI = lax.Precision.HIGH


def shifted(value, step):
    n, m = lax.axis_size("lsec"), lax.axis_size("rsec")
    pairs = [
        (i * m + j, (i + step) * m + j - step)
        for i in range(n)
        for j in range(m)
        if 0 <= i + step < n and 0 <= j - step < m
    ]
    return lax.ppermute(value, ("lsec", "rsec"), pairs)


def on_device(states, left_env, right_env, left_op, right_op, sizes_left, sizes_right):
    width = states.shape[1]
    rows = jnp.arange(width, dtype=jnp.int32)
    mask = (rows[:, None] < sizes_left[0]).astype(jnp.float32) * (
        rows[None, :] < sizes_right[0]
    ).astype(jnp.float32)
    masked = states * mask[None]
    moved = shifted(masked, 1)
    left = lax.all_gather(jnp.concatenate([left_env, left_op]), "rsec", axis=1, tiled=True)
    right = lax.all_gather(jnp.concatenate([right_env, right_op]), "lsec", axis=1, tiled=True)
    env_l, oper_l, env_r, oper_r = left[0], left[1], right[0], right[1]
    right_part = jnp.einsum("rbc,cd->rbd", masked, oper_r, precision=HI)
    source = jnp.einsum("ba,rbd->rad", oper_l, right_part, precision=HI)
    back = shifted(source, -1)
    local = jnp.einsum("ab,rbc->rac", env_l, masked, precision=HI)
    local = local + jnp.einsum("rbc,dc->rbd", masked, env_r, precision=HI)
    inner = jnp.einsum("rbc,dc->rbd", moved, oper_r, precision=HI)
    hop = jnp.einsum("ab,rbd->rad", oper_l, inner, precision=HI)
    return (local + hop + back) * mask[None]


def solution(mesh):
    in_specs = (
        P(None, "lsec", "rsec"),
        P("lsec", "rsec", None),
        P("rsec", "lsec", None),
        P("lsec", "rsec", None),
        P("rsec", "lsec", None),
        P("lsec"),
        P("rsec"),
    )
    out_specs = P(None, "lsec", "rsec")
    return jax.shard_map(
        on_device, mesh=mesh, in_specs=in_specs, out_specs=out_specs, check_vma=False
    )
```

```python
import jax
import jax.numpy as jnp
from jax import lax
from jax.experimental import pallas as pl
from jax.experimental.pallas import tpu as pltpu
from jax.sharding import PartitionSpec as P

MESH = pl.DeviceIdType.MESH
F32, BF16 = jnp.float32, jnp.bfloat16
W = 640
K = 8
C = 2 * W // K
FWD = 6
ENV, OP = 0, 1


def halves(value):
    high = value.astype(BF16)
    return high, (value - high.astype(F32)).astype(BF16)


def product(a, b, flip=False):
    dims = (((1,), (1 if flip else 0,)), ((), ()))

    def dot(u, v):
        return lax.dot_general(u, v, dims, preferred_element_type=F32)

    return dot(a[0], b[0]) + (dot(a[0], b[1]) + dot(a[1], b[0]))


def pick(cond, yes, no):
    return lax.select(cond, jnp.int32(yes), jnp.int32(no))


class Lane:
    def __init__(self, to, source, via, count, relay_from, relay_to, relay_count, last_leg):
        self.to, self.source = to, source
        self.via, self.count = via, count
        self.relay_from, self.relay_to, self.relay_count = relay_from, relay_to, relay_count
        self.last_leg = last_leg


def kernel(
    size_l, size_r, states, left_env, right_env, left_op, right_op, out,
    masked, masked_h, masked_l, hop, hop_relay, source, back, back_relay, lg, rg,
    lo_h, lo_l, lt_h, lt_l, le_h, le_l, ro_h, ro_l, re_h, re_l, mid_h, mid_l,
    hop_s, hop_r, hrel_s, hrel_r, back_s, back_r, brel_s, brel_r,
    lz_s, lz_r, ly_s, ly_r, lc_s, lc_r, rz_s, rz_r, rx_s, rx_r,
):
    i, j = lax.axis_index("lsec"), lax.axis_index("rsec")
    x, zl = lax.div(i, 4), lax.rem(i, 4)
    zh, y, c = lax.div(j, 8), lax.rem(lax.div(j, 2), 4), lax.rem(j, 2)
    up = ((i < 15) & (j > 0), i + 1, j - 1)
    down = ((i > 0) & (j < 15), i - 1, j + 1)

    h_wrap, h_cross = (zl == 3) & (c == 1) & (x < 3), (zl < 3) & (j == 8)
    h_rwrap, h_rcross = (zl == 3) & (c == 0) & (x > 0), (zl < 3) & (j == 15)
    h_lwrap, h_lcross = (zl == 0) & (c == 0) & (x > 0), (zl > 0) & (j == 7)
    lane_h = Lane(
        up, down,
        (pick(h_wrap, i + 4, i), pick(h_wrap, j - 1, 15)),
        pick(h_wrap, 2 * (x + 1), pick(h_cross, 4, 0)),
        (h_rwrap | h_rcross, pick(h_rwrap, i - 4, i), pick(h_rwrap, j + 1, 8)),
        (pick(h_rwrap, i - 3, i + 1), pick(h_rwrap, j, 7)),
        pick(h_rwrap, 2 * x, pick(h_rcross, 4, 0)),
        (h_lwrap | h_lcross, pick(h_lwrap, i + 3, i - 1), pick(h_lwrap, j, 15)),
    )
    b_wrap, b_cross = (zl == 0) & (c == 0) & (x > 0), (zl > 0) & (j == 7)
    b_rwrap, b_rcross = (zl == 0) & (c == 1) & (x < 3), (zl > 0) & (j == 0)
    b_lwrap, b_lcross = (zl == 3) & (c == 1) & (x < 3), (zl < 3) & (j == 8)
    lane_b = Lane(
        down, up,
        (pick(b_wrap, i - 4, i), pick(b_wrap, j + 1, 0)),
        pick(b_wrap, 2 * (4 - x), pick(b_cross, 4, 0)),
        (b_rwrap | b_rcross, pick(b_rwrap, i + 4, i), pick(b_rwrap, j - 1, 7)),
        (pick(b_rwrap, i + 3, i - 1), pick(b_rwrap, j, 8)),
        pick(b_rwrap, 2 * (3 - x), pick(b_rcross, 4, 0)),
        (b_lwrap | b_lcross, pick(b_lwrap, i - 3, i + 1), pick(b_lwrap, j, 0)),
    )

    other_zh = (i, lax.rem(j + 8, 16))
    other_core = (i, j + 1 - 2 * c)

    def along_y(step):
        return i, 8 * zh + 2 * lax.rem(y + step, 4) + c

    def along_z(step):
        return 4 * x + lax.rem(zl + step, 4), j

    def along_x(step):
        return lax.rem(i + 4 * step, 16), j

    bar = pltpu.get_barrier_semaphore()

    def greet(device):
        pl.semaphore_signal(bar, inc=1, device_id=device, device_id_type=MESH)

    greet(other_zh)
    greet(other_core)
    for step in (1, 2, 3):
        greet(along_y(step))
        greet(along_z(step))
        greet(along_x(step))
    expected = jnp.int32(11)
    for lane in (lane_h, lane_b):
        for ok, a, b in (lane.source, lane.relay_from, lane.last_leg):
            @pl.when(ok)
            def _():
                greet((a, b))
        expected = expected + pick(lane.to[0], 1, 0) + pick(lane.count > 0, 1, 0)
        expected = expected + pick(lane.relay_count > 0, 1, 0)
    pl.semaphore_wait(bar, expected)

    def remote(src, dst, send, recv, device):
        return pltpu.make_async_remote_copy(
            src_ref=src, dst_ref=dst, send_sem=send, recv_sem=recv,
            device_id=device, device_id_type=MESH,
        )

    left_in, right_in = (left_env, left_op), (right_env, right_op)

    def left_z(m):
        return remote(left_in[m].at[0], lg.at[m, zh, y, c], lz_s.at[m], lz_r.at[m], other_zh)

    def left_y(m, step):
        part = lg.at[m, :, y, c]
        return remote(part, part, ly_s.at[m, step - 1], ly_r.at[m, step - 1], along_y(step))

    def left_core(m):
        part = lg.at[m, :, :, c]
        return remote(part, part, lc_s.at[m], lc_r.at[m], other_core)

    def right_z(m, step):
        return remote(
            right_in[m].at[0], rg.at[m, x, zl], rz_s.at[m, step - 1], rz_r.at[m, step - 1], along_z(step)
        )

    def right_x(m, step):
        part = rg.at[m, x]
        return remote(part, part, rx_s.at[m, step - 1], rx_r.at[m, step - 1], along_x(step))

    steps = (1, 2, 3)
    for m in (OP, ENV):
        for step in steps:
            right_z(m, step).start()
        left_z(m).start()
    for m in (OP, ENV):
        lg[m, zh, y, c] = left_in[m][0]
        rg[m, x, zl] = right_in[m][0]

    def rows(k):
        return pl.ds(k * C, C)

    def straight(lane, k, src, dst, send, recv):
        return remote(src.at[rows(k)], dst.at[rows(k)], send.at[k], recv.at[k], lane.to[1:])

    def first_leg(lane, k, src, relay, send, recv):
        return remote(src.at[rows(k)], relay.at[rows(k)], send.at[k], recv.at[k], lane.via)

    def second_leg(lane, k, relay, dst, send, recv):
        return remote(relay.at[rows(k)], dst.at[rows(k)], send.at[k], recv.at[k], lane.relay_to)

    def ship(lane, k, src, dst, relay, send, recv, relay_recv):
        if k < FWD:
            @pl.when(k < lane.count)
            def _():
                first_leg(lane, k, src, relay, send, relay_recv).start()

        @pl.when(lane.to[0] & (k >= lane.count))
        def _():
            straight(lane, k, src, dst, send, recv).start()

    def ship_hop(k):
        ship(lane_h, k, masked, hop, hop_relay, hop_s, hop_r, hrel_r)

    def ship_back(k):
        ship(lane_b, k, source, back, back_relay, back_s, back_r, brel_r)

    def relay_hop(k):
        @pl.when(k < lane_h.relay_count)
        def _():
            first_leg(lane_h, k, masked, hop_relay, hop_s, hrel_r).wait_recv()
            second_leg(lane_h, k, hop_relay, hop, hrel_s, hop_r).start()

    def relay_back(k):
        @pl.when(k < lane_b.relay_count)
        def _():
            first_leg(lane_b, k, source, back_relay, back_s, brel_r).wait_recv()
            second_leg(lane_b, k, back_relay, back, brel_s, back_r).start()

    sl, sr = size_l[0], size_r[0]
    for k in range(K):
        row = lax.broadcasted_iota(jnp.int32, (C, W), 0) + (k % (K // 2)) * C
        col = lax.broadcasted_iota(jnp.int32, (C, W), 1)
        value = jnp.where((row < sl) & (col < sr), states[k * C : (k + 1) * C], 0.0)
        masked[k * C : (k + 1) * C] = value
        high, low = halves(value)
        masked_h[k * C : (k + 1) * C] = high
        masked_l[k * C : (k + 1) * C] = low
        ship_hop(k)

    @pl.when(jnp.logical_not(down[0]))
    def _():
        hop[...] = jnp.zeros_like(hop)

    @pl.when(jnp.logical_not(up[0]))
    def _():
        back[...] = jnp.zeros_like(back)

    for m in (OP, ENV):
        left_z(m).wait_recv()
        for step in steps:
            left_y(m, step).start()
        for step in steps:
            right_z(m, step).wait_recv()
        for step in steps:
            right_x(m, step).start()
    for m in (OP, ENV):
        for step in steps:
            left_y(m, step).wait_recv()
        left_core(m).start()
        relay_hop(m)

    def left_part(m, t):
        return lg[m, t // 4, t % 4].reshape(80, W)

    def right_part(m, t):
        return rg[m, t // 2, pl.ds((t % 2) * 2, 2)].reshape(80, W)

    def keep(part, m, into):
        for t in range(8):
            into[0][t * 80 : (t + 1) * 80], into[1][t * 80 : (t + 1) * 80] = halves(part(m, t))

    left_core(OP).wait_recv()
    keep(left_part, OP, (lo_h, lo_l))
    for t in range(W // 128):
        turned = lg[OP, :, :, :, :, t * 128 : (t + 1) * 128].reshape(W, 128).T
        lt_h[t * 128 : (t + 1) * 128], lt_l[t * 128 : (t + 1) * 128] = halves(turned)

    def pair(h, l, k, size):
        at = pl.ds(pl.multiple_of(k * size, size), size)
        return h[at, :], l[at, :]

    B = 320

    def left_times(l_h, l_l, m_h, m_l, k):
        return product(pair(l_h, l_l, k % 2, B), pair(m_h, m_l, k // 2, W))

    def put(k, value):
        at = pl.ds(pl.multiple_of(k * B, B), B)
        mid_h[at, :], mid_l[at, :] = halves(value)

    def at_left(k, _):
        put(k, left_times(lt_h, lt_l, masked_h, masked_l, k))
        return _

    lax.fori_loop(0, 4, at_left, 0)
    relay_hop(2)
    relay_hop(3)
    for step in steps:
        right_x(OP, step).wait_recv()
    keep(right_part, OP, (ro_h, ro_l))
    for k in range(K):
        source[rows(k), :] = product(
            (mid_h[rows(k), :], mid_l[rows(k), :]), (ro_h[...], ro_l[...])
        )
        ship_back(k)
        if k in (1, 3):
            relay_hop(4 + k // 2)

    left_core(ENV).wait_recv()
    keep(left_part, ENV, (le_h, le_l))
    for step in steps:
        right_x(ENV, step).wait_recv()
    keep(right_part, ENV, (re_h, re_l))

    def local(k, _):
        at = pl.ds(pl.multiple_of(k * B, B), B)
        out[at, :] = left_times(le_h, le_l, masked_h, masked_l, k) + product(
            pair(masked_h, masked_l, k, B), (re_h[...], re_l[...]), True
        )
        return _

    lax.fori_loop(0, 4, local, 0)
    for k in range(FWD):
        relay_back(k)

    def inner(k, _):
        at = pl.ds(pl.multiple_of(k * B, B), B)
        put(k, product(halves(hop[at, :]), (ro_h[...], ro_l[...]), True))
        return _

    def hopped(k, _):
        at = pl.ds(pl.multiple_of(k * B, B), B)
        out[at, :] += left_times(lo_h, lo_l, mid_h, mid_l, k)
        return _

    for root in range(2):
        for k in range(root * K // 2, (root + 1) * K // 2):
            @pl.when(down[0])
            def _():
                straight(lane_h, k, masked, hop, hop_s, hop_r).wait_recv()
        lax.fori_loop(2 * root, 2 * root + 2, inner, 0)
        lax.fori_loop(2 * root, 2 * root + 2, hopped, 0)

    for k in range(K):
        @pl.when(up[0])
        def _():
            straight(lane_b, k, source, back, back_s, back_r).wait_recv()

        out[rows(k), :] += back[rows(k), :]

    for m in (OP, ENV):
        left_z(m).wait_send()
        left_core(m).wait_send()
        for step in steps:
            left_y(m, step).wait_send()
            right_z(m, step).wait_send()
            right_x(m, step).wait_send()
    for k in range(K):
        @pl.when(up[0])
        def _():
            straight(lane_h, k, masked, hop, hop_s, hop_r).wait_send()

        @pl.when(down[0])
        def _():
            straight(lane_b, k, source, back, back_s, back_r).wait_send()
    for k in range(FWD):
        @pl.when(k < lane_h.relay_count)
        def _():
            second_leg(lane_h, k, hop_relay, hop, hrel_s, hop_r).wait_send()

        @pl.when(k < lane_b.relay_count)
        def _():
            second_leg(lane_b, k, back_relay, back, brel_s, back_r).wait_send()


def on_device(states, left_env, right_env, left_op, right_op, sizes_left, sizes_right):
    vmem = pl.BlockSpec(memory_space=pltpu.VMEM)
    smem = pl.BlockSpec(memory_space=pltpu.SMEM)
    whole, block = pltpu.VMEM((2 * W, W), F32), pltpu.VMEM((W, W), BF16)
    relay, half = pltpu.VMEM((FWD * C, W), F32), pltpu.VMEM((2 * W, W), BF16)
    dma = pltpu.SemaphoreType.DMA
    applied = pl.pallas_call(
        kernel,
        out_shape=jax.ShapeDtypeStruct((2 * W, W), F32),
        in_specs=[smem, smem] + [vmem] * 5,
        out_specs=vmem,
        scratch_shapes=[
            whole, half, half, whole, relay, whole, whole, relay,
            pltpu.VMEM((2, 2, 4, 2, 40, W), F32), pltpu.VMEM((2, 4, 4, 40, W), F32),
            *[block] * 10, half, half,
            dma((K,)), dma((K,)), dma((FWD,)), dma((FWD,)),
            dma((K,)), dma((K,)), dma((FWD,)), dma((FWD,)),
            dma((2,)), dma((2,)), dma((2, 3)), dma((2, 3)), dma((2,)), dma((2,)),
            dma((2, 3)), dma((2, 3)), dma((2, 3)), dma((2, 3)),
        ],
        compiler_params=pltpu.CompilerParams(
            collective_id=0, has_side_effects=True, vmem_limit_bytes=60 * 2**20
        ),
        cost_estimate=pl.CostEstimate(
            flops=24 * W**3, bytes_accessed=16 * W * W, transcendentals=0
        ),
    )(sizes_left, sizes_right, states.reshape(2 * W, W), left_env, right_env, left_op, right_op)
    places = jnp.arange(W, dtype=jnp.int32)
    mask = (places[:, None] < sizes_left[0]) & (places[None, :] < sizes_right[0])
    return jnp.where(mask[None], applied.reshape(2, W, W), 0.0)


def solution(mesh):
    in_specs = (
        P(None, "lsec", "rsec"),
        P("lsec", "rsec", None),
        P("rsec", "lsec", None),
        P("lsec", "rsec", None),
        P("rsec", "lsec", None),
        P("lsec"),
        P("rsec"),
    )
    out_specs = P(None, "lsec", "rsec")
    return jax.shard_map(
        on_device, mesh=mesh, in_specs=in_specs, out_specs=out_specs, check_vma=False
    )
```

```python
import jax
import jax.numpy as jnp
from jax import lax
from jax.experimental import pallas as pl
from jax.experimental.pallas import tpu as pltpu
from jax.sharding import PartitionSpec as P

MESH = pl.DeviceIdType.MESH
F32, BF16 = jnp.float32, jnp.bfloat16
W = 640
K = 8
C = 2 * W // K
FWD = 6
ENV, OP = 0, 1


def halves(value):
    high = value.astype(BF16)
    return high, (value - high.astype(F32)).astype(BF16)


def product(a, b, flip=False):
    dims = (((1,), (1 if flip else 0,)), ((), ()))

    def dot(u, v):
        return lax.dot_general(u, v, dims, preferred_element_type=F32)

    return dot(a[0], b[0]) + (dot(a[0], b[1]) + dot(a[1], b[0]))


def pick(cond, yes, no):
    return lax.select(cond, jnp.int32(yes), jnp.int32(no))


INSIDE = {(0, 0): 1, (0, 1): 6, (0, 2): 4, (1, 1): 1, (1, 2): 2, (3, 0): 2, (3, 1): 1}
EDGE = {
    (0, 0, 1, 1): 3, (0, 0, 2, 1): 1, (0, 1, 0, 1): 1, (0, 1, 1, 0): 1, (0, 1, 1, 1): 2, (0, 1, 2, 0): 1,
    (0, 1, 2, 1): 2, (0, 1, 3, 0): 1, (0, 1, 3, 1): 4, (1, 0, 1, 1): 6, (1, 0, 2, 1): 2, (1, 1, 0, 1): 3,
    (1, 1, 1, 1): 6, (1, 1, 2, 1): 6, (1, 1, 3, 0): 3, (1, 1, 3, 1): 6, (2, 0, 1, 0): 3, (2, 0, 1, 1): 6,
    (2, 0, 2, 0): 3, (2, 1, 0, 1): 4, (2, 1, 1, 0): 3, (2, 1, 1, 1): 6, (2, 1, 2, 0): 6, (2, 1, 2, 1): 6,
    (2, 1, 3, 0): 6, (2, 1, 3, 1): 5,
}


def detours(x, zl, j):
    total = jnp.int32(0)
    edge = 16 * x + j
    inside = 4 * j + zl
    for (px, pz, py, pc), n in EDGE.items():
        total = pick((zl == 3) & (edge == 16 * px + 8 * pz + 2 * py + pc), n, total)
    for (py, pl_), n in INSIDE.items():
        total = pick(inside == 4 * (8 + 2 * py) + pl_, n, total)
    return total


class Lane:
    def __init__(self, i, j, mirrored):
        def place(p, q):
            return (15 - p, 15 - q) if mirrored else (p, q)

        def by_way_of(p, q):
            return 4 * lax.div(p + 1, 4) + lax.rem(p, 4), 8 * lax.div(q, 8) + lax.rem(q + 7, 8)

        p, q = place(i, j)
        x, zl = lax.div(p, 4), lax.rem(p, 4)
        self.to_ok, self.to = (p < 15) & (q > 0), place(p + 1, q - 1)
        self.from_ok, self.source = (p > 0) & (q < 15), place(p - 1, q + 1)
        self.via = place(*by_way_of(p, q))
        self.count = pick(self.to_ok, detours(x, zl, q), 0)
        back_x = pick(zl == 3, x - 1, x)
        sp, sq = 4 * back_x + zl, 8 * lax.div(q, 8) + lax.rem(q + 1, 8)
        self.relay_from, self.relay_to = place(sp, sq), place(sp + 1, sq - 1)
        self.relay_count = pick((sp >= 0) & (sp < 15) & (sq > 0), detours(back_x, zl, sq), 0)
        lp, lq = lax.rem(p + 15, 16), lax.rem(q + 1, 16)
        self.last_leg = place(*by_way_of(lp, lq))
        self.last_count = pick(self.from_ok, detours(lax.div(lp, 4), lax.rem(lp, 4), lq), 0)


def kernel(
    size_l, size_r, states, left_env, right_env, left_op, right_op, out,
    masked, masked_h, masked_l, hop, hop_relay, source, back, back_relay, lg, rg,
    lo_h, lo_l, lt_h, lt_l, le_h, le_l, ro_h, ro_l, re_h, re_l, mid_h, mid_l,
    hop_s, hop_r, hrel_s, hrel_r, back_s, back_r, brel_s, brel_r,
    lz_s, lz_r, ly_s, ly_r, lc_s, lc_r, rz_s, rz_r, rx_s, rx_r,
):
    i, j = lax.axis_index("lsec"), lax.axis_index("rsec")
    x, zl = lax.div(i, 4), lax.rem(i, 4)
    zh, y, c = lax.div(j, 8), lax.rem(lax.div(j, 2), 4), lax.rem(j, 2)
    lane_h, lane_b = Lane(i, j, False), Lane(i, j, True)

    other_zh = (i, lax.rem(j + 8, 16))
    other_core = (i, j + 1 - 2 * c)

    def along_y(step):
        return i, 8 * zh + 2 * lax.rem(y + step, 4) + c

    z_next = ((zl < 3, i + 1), (zl > 0, i - 1))

    def along_x(step):
        return lax.rem(i + 4 * step, 16), j

    bar = pltpu.get_barrier_semaphore()

    def greet(device):
        pl.semaphore_signal(bar, inc=1, device_id=device, device_id_type=MESH)

    greet(other_zh)
    greet(other_core)
    for step in (1, 2, 3):
        greet(along_y(step))
        greet(along_x(step))
    expected = jnp.int32(8)
    for ok, a in z_next:
        @pl.when(ok)
        def _():
            greet((a, j))

        expected = expected + pick(ok, 1, 0)
    for lane in (lane_h, lane_b):
        for ok, device in (
            (lane.from_ok, lane.source),
            (lane.relay_count > 0, lane.relay_from),
            (lane.last_count > 0, lane.last_leg),
        ):
            @pl.when(ok)
            def _():
                greet(device)

        expected = expected + pick(lane.to_ok, 1, 0) + pick(lane.count > 0, 1, 0)
        expected = expected + pick(lane.relay_count > 0, 1, 0)
    pl.semaphore_wait(bar, expected)

    def remote(src, dst, send, recv, device):
        return pltpu.make_async_remote_copy(
            src_ref=src, dst_ref=dst, send_sem=send, recv_sem=recv,
            device_id=device, device_id_type=MESH,
        )

    left_in, right_in = (left_env, left_op), (right_env, right_op)

    def left_z(m):
        return remote(left_in[m].at[0], lg.at[m, zh, y, c], lz_s.at[m], lz_r.at[m], other_zh)

    def left_y(m, step):
        part = lg.at[m, :, y, c]
        return remote(part, part, ly_s.at[m, step - 1], ly_r.at[m, step - 1], along_y(step))

    def left_core(m):
        part = lg.at[m, :, :, c]
        return remote(part, part, lc_s.at[m], lc_r.at[m], other_core)

    def right_z(m, step, way, arriving=False):
        back = step if arriving else step - 1
        owner = zl - back if way == 0 else zl + back
        part = rg.at[m, x, owner]
        src = right_in[m].at[0] if step == 1 and not arriving else part
        copy = remote(
            src, part, rz_s.at[m, way, step - 1], rz_r.at[m, way, step - 1], (z_next[way][1], j)
        )
        return (z_next[way][0] | arriving) & (owner >= 0) & (owner <= 3), copy

    def right_z_start(m, step):
        for way in (0, 1):
            ok, copy = right_z(m, step, way)

            @pl.when(ok)
            def _():
                copy.start()

    def right_z_arrive(m, step):
        for way in (0, 1):
            ok, copy = right_z(m, step, way, True)

            @pl.when(ok)
            def _():
                copy.wait_recv()

    def right_x(m, step):
        part = rg.at[m, x]
        return remote(part, part, rx_s.at[m, step - 1], rx_r.at[m, step - 1], along_x(step))

    steps = (1, 2, 3)
    right_z_start(OP, 1)
    left_z(OP).start()
    for m in (OP, ENV):
        lg[m, zh, y, c] = left_in[m][0]
        rg[m, x, zl] = right_in[m][0]

    def rows(k):
        return pl.ds(k * C, C)

    def straight(lane, k, src, dst, send, recv):
        return remote(src.at[rows(k)], dst.at[rows(k)], send.at[k], recv.at[k], lane.to)

    def first_leg(lane, k, src, relay, send, recv):
        return remote(src.at[rows(k)], relay.at[rows(k)], send.at[k], recv.at[k], lane.via)

    def second_leg(lane, k, relay, dst, send, recv):
        return remote(relay.at[rows(k)], dst.at[rows(k)], send.at[k], recv.at[k], lane.relay_to)

    def ship(lane, k, src, dst, relay, send, recv, relay_recv):
        if k < FWD:
            @pl.when(k < lane.count)
            def _():
                first_leg(lane, k, src, relay, send, relay_recv).start()

        @pl.when(lane.to_ok & (k >= lane.count))
        def _():
            straight(lane, k, src, dst, send, recv).start()

    def ship_hop(k):
        ship(lane_h, k, masked, hop, hop_relay, hop_s, hop_r, hrel_r)

    def ship_back(k):
        ship(lane_b, k, source, back, back_relay, back_s, back_r, brel_r)

    def relay_hop(k):
        @pl.when(k < lane_h.relay_count)
        def _():
            first_leg(lane_h, k, masked, hop_relay, hop_s, hrel_r).wait_recv()
            second_leg(lane_h, k, hop_relay, hop, hrel_s, hop_r).start()

    def relay_back(k):
        @pl.when(k < lane_b.relay_count)
        def _():
            first_leg(lane_b, k, source, back_relay, back_s, brel_r).wait_recv()
            second_leg(lane_b, k, back_relay, back, brel_s, back_r).start()

    sl, sr = size_l[0], size_r[0]
    for k in range(K):
        row = lax.broadcasted_iota(jnp.int32, (C, W), 0) + (k % (K // 2)) * C
        col = lax.broadcasted_iota(jnp.int32, (C, W), 1)
        value = jnp.where((row < sl) & (col < sr), states[k * C : (k + 1) * C], 0.0)
        masked[k * C : (k + 1) * C] = value
        high, low = halves(value)
        masked_h[k * C : (k + 1) * C] = high
        masked_l[k * C : (k + 1) * C] = low
        if k < 2:
            ship_hop(k)

    @pl.when(jnp.logical_not(lane_h.from_ok))
    def _():
        hop[...] = jnp.zeros_like(hop)

    @pl.when(jnp.logical_not(lane_b.from_ok))
    def _():
        back[...] = jnp.zeros_like(back)

    def left_y_start(m):
        left_z(m).wait_recv()
        for step in steps:
            left_y(m, step).start()

    def right_x_start(m):
        right_z_arrive(m, 3)
        for step in steps:
            right_x(m, step).start()

    right_z_arrive(OP, 1)
    right_z_start(OP, 2)
    left_z(ENV).start()
    ship_hop(2)
    left_y_start(OP)
    right_z_arrive(OP, 2)
    right_z_start(OP, 3)
    right_z_start(ENV, 1)
    ship_hop(3)
    right_x_start(OP)
    ship_hop(4)
    right_z_arrive(ENV, 1)
    right_z_start(ENV, 2)
    left_y_start(ENV)
    ship_hop(5)
    relay_hop(0)
    right_z_arrive(ENV, 2)
    right_z_start(ENV, 3)
    ship_hop(6)
    ship_hop(7)
    for step in steps:
        left_y(OP, step).wait_recv()
    left_core(OP).start()
    right_x_start(ENV)
    relay_hop(1)
    for step in steps:
        left_y(ENV, step).wait_recv()
    left_core(ENV).start()

    def left_part(m, t):
        return lg[m, t // 4, t % 4].reshape(80, W)

    def right_part(m, t):
        return rg[m, t // 2, pl.ds((t % 2) * 2, 2)].reshape(80, W)

    def keep(part, m, into):
        for t in range(8):
            into[0][t * 80 : (t + 1) * 80], into[1][t * 80 : (t + 1) * 80] = halves(part(m, t))

    left_core(OP).wait_recv()
    keep(left_part, OP, (lo_h, lo_l))
    for t in range(W // 128):
        turned = lg[OP, :, :, :, :, t * 128 : (t + 1) * 128].reshape(W, 128).T
        lt_h[t * 128 : (t + 1) * 128], lt_l[t * 128 : (t + 1) * 128] = halves(turned)

    def pair(h, l, k, size):
        at = pl.ds(pl.multiple_of(k * size, size), size)
        return h[at, :], l[at, :]

    B = 320

    def left_times(l_h, l_l, m_h, m_l, k):
        return product(pair(l_h, l_l, k % 2, B), pair(m_h, m_l, k // 2, W))

    def put(k, value):
        at = pl.ds(pl.multiple_of(k * B, B), B)
        mid_h[at, :], mid_l[at, :] = halves(value)

    def at_left(k, _):
        put(k, left_times(lt_h, lt_l, masked_h, masked_l, k))
        return _

    lax.fori_loop(0, 4, at_left, 0)
    relay_hop(2)
    relay_hop(3)
    for step in steps:
        right_x(OP, step).wait_recv()
    keep(right_part, OP, (ro_h, ro_l))
    for k in range(K):
        source[rows(k), :] = product(
            (mid_h[rows(k), :], mid_l[rows(k), :]), (ro_h[...], ro_l[...])
        )
        ship_back(k)
        if k in (1, 3):
            relay_hop(4 + k // 2)

    left_core(ENV).wait_recv()
    keep(left_part, ENV, (le_h, le_l))
    for step in steps:
        right_x(ENV, step).wait_recv()
    keep(right_part, ENV, (re_h, re_l))

    def local(k, _):
        at = pl.ds(pl.multiple_of(k * B, B), B)
        out[at, :] = left_times(le_h, le_l, masked_h, masked_l, k) + product(
            pair(masked_h, masked_l, k, B), (re_h[...], re_l[...]), True
        )
        return _

    lax.fori_loop(0, 4, local, 0)
    for k in range(FWD):
        relay_back(k)

    def hopped(k, _):
        at = pl.ds(pl.multiple_of(k * B, B), B)
        out[at, :] += left_times(lo_h, lo_l, mid_h, mid_l, k)
        return _

    for k in range(K):
        @pl.when(lane_h.from_ok)
        def _():
            straight(lane_h, k, masked, hop, hop_s, hop_r).wait_recv()

        mid_h[rows(k), :], mid_l[rows(k), :] = halves(
            product(halves(hop[rows(k), :]), (ro_h[...], ro_l[...]), True)
        )
        if k % (K // 2) == K // 2 - 1:
            lax.fori_loop(k // 2 - 1, k // 2 + 1, hopped, 0)

    for k in range(K):
        @pl.when(lane_b.from_ok)
        def _():
            straight(lane_b, k, source, back, back_s, back_r).wait_recv()

        out[rows(k), :] += back[rows(k), :]

    for m in (OP, ENV):
        left_z(m).wait_send()
        left_core(m).wait_send()
        for step in steps:
            left_y(m, step).wait_send()
            right_x(m, step).wait_send()
            for way in (0, 1):
                ok, copy = right_z(m, step, way)

                @pl.when(ok)
                def _():
                    copy.wait_send()
    for k in range(K):
        @pl.when(lane_h.to_ok)
        def _():
            straight(lane_h, k, masked, hop, hop_s, hop_r).wait_send()

        @pl.when(lane_b.to_ok)
        def _():
            straight(lane_b, k, source, back, back_s, back_r).wait_send()
    for k in range(FWD):
        @pl.when(k < lane_h.relay_count)
        def _():
            second_leg(lane_h, k, hop_relay, hop, hrel_s, hop_r).wait_send()

        @pl.when(k < lane_b.relay_count)
        def _():
            second_leg(lane_b, k, back_relay, back, brel_s, back_r).wait_send()


def on_device(states, left_env, right_env, left_op, right_op, sizes_left, sizes_right):
    vmem = pl.BlockSpec(memory_space=pltpu.VMEM)
    smem = pl.BlockSpec(memory_space=pltpu.SMEM)
    whole, block = pltpu.VMEM((2 * W, W), F32), pltpu.VMEM((W, W), BF16)
    relay, half = pltpu.VMEM((FWD * C, W), F32), pltpu.VMEM((2 * W, W), BF16)
    dma = pltpu.SemaphoreType.DMA
    applied = pl.pallas_call(
        kernel,
        out_shape=jax.ShapeDtypeStruct((2 * W, W), F32),
        in_specs=[smem, smem] + [vmem] * 5,
        out_specs=vmem,
        scratch_shapes=[
            whole, half, half, whole, relay, whole, whole, relay,
            pltpu.VMEM((2, 2, 4, 2, 40, W), F32), pltpu.VMEM((2, 4, 4, 40, W), F32),
            *[block] * 10, half, half,
            dma((K,)), dma((K,)), dma((FWD,)), dma((FWD,)),
            dma((K,)), dma((K,)), dma((FWD,)), dma((FWD,)),
            dma((2,)), dma((2,)), dma((2, 3)), dma((2, 3)), dma((2,)), dma((2,)),
            dma((2, 2, 3)), dma((2, 2, 3)), dma((2, 3)), dma((2, 3)),
        ],
        compiler_params=pltpu.CompilerParams(
            collective_id=0, has_side_effects=True, vmem_limit_bytes=48 * 2**20
        ),
        cost_estimate=pl.CostEstimate(
            flops=24 * W**3, bytes_accessed=16 * W * W, transcendentals=0
        ),
    )(sizes_left, sizes_right, states.reshape(2 * W, W), left_env, right_env, left_op, right_op)
    places = jnp.arange(W, dtype=jnp.int32)
    mask = (places[:, None] < sizes_left[0]) & (places[None, :] < sizes_right[0])
    return jnp.where(mask[None], applied.reshape(2, W, W), 0.0)


def solution(mesh):
    in_specs = (
        P(None, "lsec", "rsec"),
        P("lsec", "rsec", None),
        P("rsec", "lsec", None),
        P("lsec", "rsec", None),
        P("rsec", "lsec", None),
        P("lsec"),
        P("rsec"),
    )
    out_specs = P(None, "lsec", "rsec")
    return jax.shard_map(
        on_device, mesh=mesh, in_specs=in_specs, out_specs=out_specs, check_vma=False
    )
```

```python
import jax
import jax.numpy as jnp
from jax import lax
from jax.experimental import pallas as pl
from jax.experimental.pallas import tpu as pltpu
from jax.sharding import PartitionSpec as P

MESH = pl.DeviceIdType.MESH
F32, BF16 = jnp.float32, jnp.bfloat16
W = 640
K = 8
C = 2 * W // K
FWD = 6
ENV, OP = 0, 1


def halves(value):
    high = value.astype(BF16)
    return high, (value - high.astype(F32)).astype(BF16)


def product(a, b, flip=False):
    dims = (((1,), (1 if flip else 0,)), ((), ()))

    def dot(u, v):
        return lax.dot_general(u, v, dims, preferred_element_type=F32)

    return dot(a[0], b[0]) + (dot(a[0], b[1]) + dot(a[1], b[0]))


def pick(cond, yes, no):
    return lax.select(cond, jnp.int32(yes), jnp.int32(no))


class Lane:
    def __init__(self, to, source, via, count, relay_from, relay_to, relay_count, last_leg):
        self.to, self.source = to, source
        self.via, self.count = via, count
        self.relay_from, self.relay_to, self.relay_count = relay_from, relay_to, relay_count
        self.last_leg = last_leg


def kernel(
    size_l, size_r, states, left_env, right_env, left_op, right_op, out,
    masked, masked_h, masked_l, hop, hop_relay, source, back, back_relay, lg, rg,
    lo_h, lo_l, lt_h, lt_l, le_h, le_l, ro_h, ro_l, re_h, re_l, mid_h, mid_l,
    hop_s, hop_r, hrel_s, hrel_r, back_s, back_r, brel_s, brel_r,
    lz_s, lz_r, ly_s, ly_r, lc_s, lc_r, rz_s, rz_r, rx_s, rx_r,
):
    i, j = lax.axis_index("lsec"), lax.axis_index("rsec")
    x, zl = lax.div(i, 4), lax.rem(i, 4)
    zh, y, c = lax.div(j, 8), lax.rem(lax.div(j, 2), 4), lax.rem(j, 2)
    up = ((i < 15) & (j > 0), i + 1, j - 1)
    down = ((i > 0) & (j < 15), i - 1, j + 1)

    h_wrap, h_cross = (zl == 3) & (c == 1) & (x < 3), (zl < 3) & (j == 8)
    h_rwrap, h_rcross = (zl == 3) & (c == 0) & (x > 0), (zl < 3) & (j == 15)
    h_lwrap, h_lcross = (zl == 0) & (c == 0) & (x > 0), (zl > 0) & (j == 7)
    lane_h = Lane(
        up, down,
        (pick(h_wrap, i + 4, i), pick(h_wrap, j - 1, 15)),
        pick(h_wrap, 2 * (x + 1), pick(h_cross, 4, 0)),
        (h_rwrap | h_rcross, pick(h_rwrap, i - 4, i), pick(h_rwrap, j + 1, 8)),
        (pick(h_rwrap, i - 3, i + 1), pick(h_rwrap, j, 7)),
        pick(h_rwrap, 2 * x, pick(h_rcross, 4, 0)),
        (h_lwrap | h_lcross, pick(h_lwrap, i + 3, i - 1), pick(h_lwrap, j, 15)),
    )
    b_wrap, b_cross = (zl == 0) & (c == 0) & (x > 0), (zl > 0) & (j == 7)
    b_rwrap, b_rcross = (zl == 0) & (c == 1) & (x < 3), (zl > 0) & (j == 0)
    b_lwrap, b_lcross = (zl == 3) & (c == 1) & (x < 3), (zl < 3) & (j == 8)
    lane_b = Lane(
        down, up,
        (pick(b_wrap, i - 4, i), pick(b_wrap, j + 1, 0)),
        pick(b_wrap, 2 * (4 - x), pick(b_cross, 4, 0)),
        (b_rwrap | b_rcross, pick(b_rwrap, i + 4, i), pick(b_rwrap, j - 1, 7)),
        (pick(b_rwrap, i + 3, i - 1), pick(b_rwrap, j, 8)),
        pick(b_rwrap, 2 * (3 - x), pick(b_rcross, 4, 0)),
        (b_lwrap | b_lcross, pick(b_lwrap, i - 3, i + 1), pick(b_lwrap, j, 0)),
    )

    other_zh = (i, lax.rem(j + 8, 16))
    other_core = (i, j + 1 - 2 * c)

    def along_y(step):
        return i, 8 * zh + 2 * lax.rem(y + step, 4) + c

    def along_z(step):
        return 4 * x + lax.rem(zl + step, 4), j

    def along_x(step):
        return lax.rem(i + 4 * step, 16), j

    bar = pltpu.get_barrier_semaphore()

    def greet(device):
        pl.semaphore_signal(bar, inc=1, device_id=device, device_id_type=MESH)

    greet(other_zh)
    greet(other_core)
    for step in (1, 2, 3):
        greet(along_y(step))
        greet(along_z(step))
        greet(along_x(step))
    expected = jnp.int32(11)
    for lane in (lane_h, lane_b):
        for ok, a, b in (lane.source, lane.relay_from, lane.last_leg):
            @pl.when(ok)
            def _():
                greet((a, b))
        expected = expected + pick(lane.to[0], 1, 0) + pick(lane.count > 0, 1, 0)
        expected = expected + pick(lane.relay_count > 0, 1, 0)
    pl.semaphore_wait(bar, expected)

    def remote(src, dst, send, recv, device):
        return pltpu.make_async_remote_copy(
            src_ref=src, dst_ref=dst, send_sem=send, recv_sem=recv,
            device_id=device, device_id_type=MESH,
        )

    left_in, right_in = (left_env, left_op), (right_env, right_op)

    def left_z(m):
        return remote(left_in[m].at[0], lg.at[m, zh, y, c], lz_s.at[m], lz_r.at[m], other_zh)

    def left_y(m, step):
        part = lg.at[m, :, y, c]
        return remote(part, part, ly_s.at[m, step - 1], ly_r.at[m, step - 1], along_y(step))

    def left_core(m):
        part = lg.at[m, :, :, c]
        return remote(part, part, lc_s.at[m], lc_r.at[m], other_core)

    def right_z(m, step):
        return remote(
            right_in[m].at[0], rg.at[m, x, zl], rz_s.at[m, step - 1], rz_r.at[m, step - 1], along_z(step)
        )

    def right_x(m, step):
        part = rg.at[m, x]
        return remote(part, part, rx_s.at[m, step - 1], rx_r.at[m, step - 1], along_x(step))

    steps = (1, 2, 3)
    for m in (OP, ENV):
        for step in steps:
            right_z(m, step).start()
        left_z(m).start()
    for m in (OP, ENV):
        lg[m, zh, y, c] = left_in[m][0]
        rg[m, x, zl] = right_in[m][0]

    def rows(k):
        return pl.ds(k * C, C)

    def straight(lane, k, src, dst, send, recv):
        return remote(src.at[rows(k)], dst.at[rows(k)], send.at[k], recv.at[k], lane.to[1:])

    def first_leg(lane, k, src, relay, send, recv):
        return remote(src.at[rows(k)], relay.at[rows(k)], send.at[k], recv.at[k], lane.via)

    def second_leg(lane, k, relay, dst, send, recv):
        return remote(relay.at[rows(k)], dst.at[rows(k)], send.at[k], recv.at[k], lane.relay_to)

    def ship_straight(lane, k, src, dst, send, recv):
        @pl.when(lane.to[0] & (k >= lane.count))
        def _():
            straight(lane, k, src, dst, send, recv).start()

    def ship_first_leg(lane, k, src, relay, send, relay_recv):
        @pl.when(k < lane.count)
        def _():
            first_leg(lane, k, src, relay, send, relay_recv).start()

    def ship_back(k):
        if k < FWD:
            ship_first_leg(lane_b, k, source, back_relay, back_s, brel_r)
        ship_straight(lane_b, k, source, back, back_s, back_r)

    def relay_hop(k):
        @pl.when(k < lane_h.relay_count)
        def _():
            first_leg(lane_h, k, masked, hop_relay, hop_s, hrel_r).wait_recv()
            second_leg(lane_h, k, hop_relay, hop, hrel_s, hop_r).start()

    def relay_back(k):
        @pl.when(k < lane_b.relay_count)
        def _():
            first_leg(lane_b, k, source, back_relay, back_s, brel_r).wait_recv()
            second_leg(lane_b, k, back_relay, back, brel_s, back_r).start()

    sl, sr = size_l[0], size_r[0]
    for k in range(K):
        row = lax.broadcasted_iota(jnp.int32, (C, W), 0) + (k % (K // 2)) * C
        col = lax.broadcasted_iota(jnp.int32, (C, W), 1)
        value = jnp.where((row < sl) & (col < sr), states[k * C : (k + 1) * C], 0.0)
        masked[k * C : (k + 1) * C] = value
        high, low = halves(value)
        masked_h[k * C : (k + 1) * C] = high
        masked_l[k * C : (k + 1) * C] = low
        ship_straight(lane_h, k, masked, hop, hop_s, hop_r)

    @pl.when(jnp.logical_not(down[0]))
    def _():
        hop[...] = jnp.zeros_like(hop)

    @pl.when(jnp.logical_not(up[0]))
    def _():
        back[...] = jnp.zeros_like(back)

    for m in (OP, ENV):
        left_z(m).wait_recv()
        for step in steps:
            left_y(m, step).start()
        for step in steps:
            right_z(m, step).wait_recv()
        for step in steps:
            right_x(m, step).start()
        if m == OP:
            for k in range(FWD):
                ship_first_leg(lane_h, k, masked, hop_relay, hop_s, hrel_r)
    for m in (OP, ENV):
        for step in steps:
            left_y(m, step).wait_recv()
        left_core(m).start()

    def left_part(m, t):
        return lg[m, t // 4, t % 4].reshape(80, W)

    def right_part(m, t):
        return rg[m, t // 2, pl.ds((t % 2) * 2, 2)].reshape(80, W)

    def keep(part, m, into):
        for t in range(8):
            into[0][t * 80 : (t + 1) * 80], into[1][t * 80 : (t + 1) * 80] = halves(part(m, t))

    left_core(OP).wait_recv()
    keep(left_part, OP, (lo_h, lo_l))
    for t in range(W // 128):
        turned = lg[OP, :, :, :, :, t * 128 : (t + 1) * 128].reshape(W, 128).T
        lt_h[t * 128 : (t + 1) * 128], lt_l[t * 128 : (t + 1) * 128] = halves(turned)

    def pair(h, l, k, size):
        at = pl.ds(pl.multiple_of(k * size, size), size)
        return h[at, :], l[at, :]

    B = 320

    def left_times(l_h, l_l, m_h, m_l, k):
        return product(pair(l_h, l_l, k % 2, B), pair(m_h, m_l, k // 2, W))

    def put(k, value):
        at = pl.ds(pl.multiple_of(k * B, B), B)
        mid_h[at, :], mid_l[at, :] = halves(value)

    def at_left(k, _):
        put(k, left_times(lt_h, lt_l, masked_h, masked_l, k))
        return _

    lax.fori_loop(0, 4, at_left, 0)
    relay_hop(0)
    relay_hop(1)
    for step in steps:
        right_x(OP, step).wait_recv()
    keep(right_part, OP, (ro_h, ro_l))
    for k in range(K):
        source[rows(k), :] = product(
            (mid_h[rows(k), :], mid_l[rows(k), :]), (ro_h[...], ro_l[...])
        )
        ship_back(k)
        if 2 <= k < FWD:
            relay_hop(k)

    left_core(ENV).wait_recv()
    keep(left_part, ENV, (le_h, le_l))
    for step in steps:
        right_x(ENV, step).wait_recv()
    keep(right_part, ENV, (re_h, re_l))

    def local(k, _):
        at = pl.ds(pl.multiple_of(k * B, B), B)
        out[at, :] = left_times(le_h, le_l, masked_h, masked_l, k) + product(
            pair(masked_h, masked_l, k, B), (re_h[...], re_l[...]), True
        )
        return _

    for k in range(FWD):
        relay_back(k)
    lax.fori_loop(0, 4, local, 0)

    def hopped(k, _):
        at = pl.ds(pl.multiple_of(k * B, B), B)
        out[at, :] += left_times(lo_h, lo_l, mid_h, mid_l, k)
        return _

    for k in range(K):
        @pl.when(down[0])
        def _():
            straight(lane_h, k, masked, hop, hop_s, hop_r).wait_recv()

        mid_h[rows(k), :], mid_l[rows(k), :] = halves(
            product(halves(hop[rows(k), :]), (ro_h[...], ro_l[...]), True)
        )
        if k % (K // 2) == K // 2 - 1:
            lax.fori_loop(k // 2 - 1, k // 2 + 1, hopped, 0)

    for k in range(K):
        @pl.when(up[0])
        def _():
            straight(lane_b, k, source, back, back_s, back_r).wait_recv()

        out[rows(k), :] += back[rows(k), :]

    for m in (OP, ENV):
        left_z(m).wait_send()
        left_core(m).wait_send()
        for step in steps:
            left_y(m, step).wait_send()
            right_z(m, step).wait_send()
            right_x(m, step).wait_send()
    for k in range(K):
        @pl.when(up[0])
        def _():
            straight(lane_h, k, masked, hop, hop_s, hop_r).wait_send()

        @pl.when(down[0])
        def _():
            straight(lane_b, k, source, back, back_s, back_r).wait_send()
    for k in range(FWD):
        @pl.when(k < lane_h.relay_count)
        def _():
            second_leg(lane_h, k, hop_relay, hop, hrel_s, hop_r).wait_send()

        @pl.when(k < lane_b.relay_count)
        def _():
            second_leg(lane_b, k, back_relay, back, brel_s, back_r).wait_send()


def on_device(states, left_env, right_env, left_op, right_op, sizes_left, sizes_right):
    vmem = pl.BlockSpec(memory_space=pltpu.VMEM)
    smem = pl.BlockSpec(memory_space=pltpu.SMEM)
    whole, block = pltpu.VMEM((2 * W, W), F32), pltpu.VMEM((W, W), BF16)
    relay, half = pltpu.VMEM((FWD * C, W), F32), pltpu.VMEM((2 * W, W), BF16)
    dma = pltpu.SemaphoreType.DMA
    applied = pl.pallas_call(
        kernel,
        out_shape=jax.ShapeDtypeStruct((2 * W, W), F32),
        in_specs=[smem, smem] + [vmem] * 5,
        out_specs=vmem,
        scratch_shapes=[
            whole, half, half, whole, relay, whole, whole, relay,
            pltpu.VMEM((2, 2, 4, 2, 40, W), F32), pltpu.VMEM((2, 4, 4, 40, W), F32),
            *[block] * 10, half, half,
            dma((K,)), dma((K,)), dma((FWD,)), dma((FWD,)),
            dma((K,)), dma((K,)), dma((FWD,)), dma((FWD,)),
            dma((2,)), dma((2,)), dma((2, 3)), dma((2, 3)), dma((2,)), dma((2,)),
            dma((2, 3)), dma((2, 3)), dma((2, 3)), dma((2, 3)),
        ],
        compiler_params=pltpu.CompilerParams(
            collective_id=0, has_side_effects=True, vmem_limit_bytes=48 * 2**20
        ),
        cost_estimate=pl.CostEstimate(
            flops=24 * W**3, bytes_accessed=16 * W * W, transcendentals=0
        ),
    )(sizes_left, sizes_right, states.reshape(2 * W, W), left_env, right_env, left_op, right_op)
    places = jnp.arange(W, dtype=jnp.int32)
    mask = (places[:, None] < sizes_left[0]) & (places[None, :] < sizes_right[0])
    return jnp.where(mask[None], applied.reshape(2, W, W), 0.0)


def solution(mesh):
    in_specs = (
        P(None, "lsec", "rsec"),
        P("lsec", "rsec", None),
        P("rsec", "lsec", None),
        P("lsec", "rsec", None),
        P("rsec", "lsec", None),
        P("lsec"),
        P("rsec"),
    )
    out_specs = P(None, "lsec", "rsec")
    return jax.shard_map(
        on_device, mesh=mesh, in_specs=in_specs, out_specs=out_specs, check_vma=False
    )
```
